1024 devices in a mesh: hid: 64 (over x, z_lo), wid: 16 (over y, z_hi, core).
Axes of the slice: x: 4, y: 4, z: 32 (z_hi: 2, z_lo: 16; z = z_hi * 16 + z_lo), core: 2. Of those that a mesh axis runs over, the one named last changes fastest.
Arguments:
- inputs: bfloat16 [384, 8192], P('wid'), may hold values from -6 to 6
- out_grad: bfloat16 [384, 8192], P('wid'), may hold values from -6 to 6
- gate_weight: bfloat16 [8192, 28672], P('wid', 'hid'), may hold values from -0.0625 to 0.0625
- up_weight: bfloat16 [8192, 28672], P('wid', 'hid'), may hold values from -0.0625 to 0.0625
- down_weight: bfloat16 [28672, 8192], P('hid', 'wid'), may hold values from -0.03125 to 0.03125
Outputs:
- input_grad: bfloat16 [384, 8192], P('hid', 'wid')
- gate_grad: bfloat16 [8192, 28672], P('wid', 'hid')
- up_grad: bfloat16 [8192, 28672], P('wid', 'hid')
- down_grad: bfloat16 [28672, 8192], P('hid', 'wid')
The draws below stay inside these ranges and needn't reach their ends.
All inputs are finite; a program needn't handle non-finite values.
Results may differ from the reference program's by a relative error of at most 0.005.
Values may be sent and summed in bfloat16 or wider, within the bound.
No kernel may reach another device: no remote copies, remote signals or barrier semaphores. Data moves between devices by JAX's collectives and lax.ppermute only.
A program may use at most 32 MiB of HBM per device.

```python
import jax
import jax.numpy as jnp
from jax import lax

D = 8192
FF = 28672
TOKENS = 384


def levels(key, dims, split, least, top_value):
    loudness, own = 1.0, jax.random.fold_in(key, 6)
    for dim, shards_of in split:
        draws = jnp.exp(jax.random.uniform(jax.random.fold_in(own, dim), (shards_of,), jnp.float32, least / len(split), top_value / len(split)))
        loudness = loudness * jnp.repeat(draws, dims[dim] // shards_of).reshape([-1 if axis == dim else 1 for axis in range(len(dims))])
    return loudness


def normal_values(own_key, dims, width, bound, pieces=(), dtype=jnp.bfloat16):
    drawn = jax.random.normal(own_key, dims, jnp.float32) * width
    if len(pieces) > 0:
        drawn = levels(own_key, dims, pieces, -0.22, 0.18) * drawn
    return jnp.clip(drawn, min=-bound, max=bound).astype(dtype)


def setup_inputs(seed: int = 0) -> dict:
    arg_keys = jax.random.split(jax.random.key(seed), 6)
    inputs = normal_values(arg_keys[0], (TOKENS, D), 1.0, 6.0, ((0, 16),))
    out_grad = normal_values(arg_keys[1], (TOKENS, D), 1.0, 6.0, ((0, 16),))
    gate_weight = normal_values(arg_keys[2], (D, FF), D ** -0.5, 0.0625, ((0, 16), (1, 64)))
    up_weight = normal_values(arg_keys[3], (D, FF), D ** -0.5, 0.0625, ((0, 16), (1, 64)))
    down_weight = normal_values(arg_keys[4], (FF, D), FF ** -0.5, 0.03125, ((0, 64), (1, 16)))
    return {"inputs": inputs, "out_grad": out_grad, "gate_weight": gate_weight, "up_weight": up_weight, "down_weight": down_weight}


def trans_dot(left, right):
    return lax.dot_general(left, right, (((0,), (0,)), ((), ())), preferred_element_type=jnp.float32)


def dot_trans(left, right):
    return lax.dot_general(left, right, (((1,), (1,)), ((), ())), preferred_element_type=jnp.float32)


def reference(inputs, out_grad, gate_weight, up_weight, down_weight):
    gate = jnp.dot(inputs, gate_weight, preferred_element_type=jnp.float32)
    up = jnp.dot(inputs, up_weight, preferred_element_type=jnp.float32)
    hidden_grad = dot_trans(out_grad, down_weight)
    sig = jax.nn.sigmoid(gate)
    hidden = (gate * sig * up).astype(jnp.bfloat16)
    gate_delta = (hidden_grad * up * sig * (1.0 + gate * (1.0 - sig))).astype(jnp.bfloat16)
    up_delta = (hidden_grad * gate * sig).astype(jnp.bfloat16)
    down_grad = trans_dot(hidden, out_grad).astype(jnp.bfloat16)
    gate_grad = trans_dot(inputs, gate_delta).astype(jnp.bfloat16)
    up_grad = trans_dot(inputs, up_delta).astype(jnp.bfloat16)
    input_grad = (dot_trans(gate_delta, gate_weight) + dot_trans(up_delta, up_weight)).astype(jnp.bfloat16)
    return input_grad, gate_grad, up_grad, down_grad
```

```python
import jax
import jax.numpy as jnp
from jax import lax
from jax.sharding import Mesh, PartitionSpec as P

AXES = ("x", "zlo", "y", "zhi", "core")
HID = ("x", "zlo")
WID = ("y", "zhi", "core")
BF16 = jnp.bfloat16
F32 = jnp.float32


def trans_dot(left, right):
    return lax.dot_general(
        left, right, (((0,), (0,)), ((), ())), preferred_element_type=F32
    )


def dot_trans(left, right):
    return lax.dot_general(
        left, right, (((1,), (1,)), ((), ())), preferred_element_type=F32
    )


def nonlinear(gate, up, hidden_grad):
    sig = jax.nn.sigmoid(gate)
    hidden = (gate * sig * up).astype(BF16)
    gate_delta = (hidden_grad * up * sig * (1.0 + gate * (1.0 - sig))).astype(BF16)
    up_delta = (hidden_grad * gate * sig).astype(BF16)
    return jnp.stack([hidden, gate_delta, up_delta])


def exchange(value, axis):
    return lax.all_to_all(value, axis, 0, 0, tiled=True)


def flip(value, axis):
    return lax.ppermute(value, axis, [(0, 1), (1, 0)])


def spread(value, axis, size):
    return exchange(jnp.broadcast_to(value[None], (size, *value.shape)), axis)


def make_shards(sizes):
    nx, nz, ny, nc = sizes["x"], sizes["zlo"], sizes["y"], sizes["core"]
    nw = ny * sizes["zhi"] * nc

    def shards(inputs, out_grad, gate_weight, up_weight, down_weight):
        at_x = lax.axis_index("x")
        at_core = lax.axis_index("core")
        own, width = inputs.shape
        cols = width // (nw * nx)
        tokens = own * nw
        hid = gate_weight.shape[1]

        both = jnp.stack([inputs, out_grad]).reshape(2, own, nw, nx, cols)
        quarter = lax.dynamic_index_in_dim(both, at_x, 3, keepdims=False)
        quarter = exchange(quarter.transpose(2, 0, 1, 3), WID)
        whole = spread(quarter, "x", nx)
        whole = whole.transpose(2, 1, 3, 0, 4).reshape(2, tokens, nx * cols)
        cols_in, cols_grad = whole[0], whole[1]

        gate_part = jnp.dot(cols_in, gate_weight, preferred_element_type=F32)
        up_part = jnp.dot(cols_in, up_weight, preferred_element_type=F32)
        grad_part = dot_trans(cols_grad, down_weight)
        block = tokens // (nc * ny)
        parts = jnp.stack([gate_part, up_part, grad_part]).reshape(3, nc, ny, block, hid)

        keep = lax.dynamic_index_in_dim(parts, at_core, 1, keepdims=False)
        give = lax.dynamic_index_in_dim(parts, 1 - at_core, 1, keepdims=False)
        chip = keep + flip(give, "core")
        chip = exchange(chip.transpose(1, 0, 2, 3), "y")
        half = jnp.sum(chip, axis=0)
        full = half + flip(half.astype(BF16), "zhi").astype(F32)

        deltas = spread(nonlinear(full[0], full[1], full[2]), "y", ny)
        other = flip(deltas, "core")
        first = jnp.where(at_core == 0, deltas, other)
        second = jnp.where(at_core == 0, other, deltas)
        deltas = jnp.stack([first, second]).transpose(2, 0, 1, 3, 4).reshape(3, tokens, hid)
        hidden, gate_delta, up_delta = deltas[0], deltas[1], deltas[2]

        summed = dot_trans(gate_delta, gate_weight) + dot_trans(up_delta, up_weight)
        wide = summed.shape[1]
        summed = exchange(summed.reshape(nx, tokens // nx, wide), "x")
        summed = jnp.sum(summed, axis=0).astype(BF16)
        summed = exchange(summed.reshape(nz, tokens // (nx * nz), wide), "zlo")
        summed = jnp.sum(summed.astype(F32), axis=0).astype(BF16)

        down_grad = trans_dot(hidden, cols_grad).astype(BF16)
        gate_grad = trans_dot(cols_in, gate_delta).astype(BF16)
        up_grad = trans_dot(cols_in, up_delta).astype(BF16)
        return (summed, gate_grad, up_grad, down_grad)

    return shards


def build(mesh):
    return jax.shard_map(
        make_shards(mesh.shape),
        mesh=mesh,
        in_specs=(P(WID, None), P(WID, None), P(WID, HID), P(WID, HID), P(HID, WID)),
        out_specs=(P(HID, WID), P(WID, HID), P(WID, HID), P(HID, WID)),
        check_vma=False,
    )


def solution(mesh):
    return build(Mesh(mesh.devices.reshape(4, 16, 4, 2, 2), AXES))
```

```python
import jax
import jax.numpy as jnp
from jax import lax
from jax.sharding import Mesh, PartitionSpec as P

AXES = ("x", "zb", "zm", "zn", "y", "zhi", "core")
HID = ("x", "zb", "zm", "zn")
WID = ("y", "zhi", "core")
BF16 = jnp.bfloat16
F32 = jnp.float32


def trans_dot(left, right):
    return lax.dot_general(
        left, right, (((0,), (0,)), ((), ())), preferred_element_type=F32
    )


def dot_trans(left, right):
    return lax.dot_general(
        left, right, (((1,), (1,)), ((), ())), preferred_element_type=F32
    )


def nonlinear(gate, up, hidden_grad):
    sig = jax.nn.sigmoid(gate)
    hidden = (gate * sig * up).astype(BF16)
    gate_delta = (hidden_grad * up * sig * (1.0 + gate * (1.0 - sig))).astype(BF16)
    up_delta = (hidden_grad * gate * sig).astype(BF16)
    return jnp.stack([hidden, gate_delta, up_delta])


def exchange(value, axis):
    return lax.all_to_all(value, axis, 0, 0, tiled=True)


def flip(value, axis):
    return lax.ppermute(value, axis, [(0, 1), (1, 0)])


def spread(value, axis, size):
    return exchange(jnp.broadcast_to(value[None], (size, *value.shape)), axis)


def near_groups(ny, nc):
    return [
        [((g ^ h) * ny + y) * 2 * nc + h * nc + c for y in range(ny) for h in range(2) for c in range(nc)]
        for g in range(2)
    ]


def make_shards(sizes):
    nx, ny, nc = sizes["x"], sizes["y"], sizes["core"]
    far, near = sizes["zb"] * sizes["zm"], sizes["zn"]
    nw = ny * sizes["zhi"] * nc
    groups = near_groups(ny, nc)

    def shards(inputs, out_grad, gate_weight, up_weight, down_weight):
        at_x = lax.axis_index("x")
        at_core = lax.axis_index("core")
        own, width = inputs.shape
        cols = width // (nw * nx)
        tokens = own * nw
        hid = gate_weight.shape[1]

        both = jnp.stack([inputs, out_grad]).reshape(2, own, nw, nx, cols)
        quarter = lax.dynamic_index_in_dim(both, at_x, 3, keepdims=False)
        quarter = lax.all_to_all(
            quarter.transpose(2, 0, 1, 3), ("zb", *WID), 0, 0, axis_index_groups=groups, tiled=True
        )
        whole = spread(quarter, "x", nx)
        whole = whole.transpose(2, 1, 3, 0, 4).reshape(2, tokens, nx * cols)
        cols_in, cols_grad = whole[0], whole[1]

        gate_part = jnp.dot(cols_in, gate_weight, preferred_element_type=F32)
        up_part = jnp.dot(cols_in, up_weight, preferred_element_type=F32)
        grad_part = dot_trans(cols_grad, down_weight)
        block = tokens // (nc * ny)
        parts = jnp.stack([gate_part, up_part, grad_part]).reshape(3, nc, ny, block, hid)

        keep = lax.dynamic_index_in_dim(parts, at_core, 1, keepdims=False)
        give = lax.dynamic_index_in_dim(parts, 1 - at_core, 1, keepdims=False)
        chip = keep + flip(give, "core")
        chip = exchange(chip.transpose(1, 0, 2, 3), "y")
        half = jnp.sum(chip, axis=0)
        full = half + flip(half.astype(BF16), "zhi").astype(F32)

        deltas = spread(nonlinear(full[0], full[1], full[2]), "y", ny)
        other = flip(deltas, "core")
        first = jnp.where(at_core == 0, deltas, other)
        second = jnp.where(at_core == 0, other, deltas)
        deltas = jnp.stack([first, second]).transpose(2, 0, 1, 3, 4).reshape(3, tokens, hid)
        hidden, gate_delta, up_delta = deltas[0], deltas[1], deltas[2]

        summed = dot_trans(gate_delta, gate_weight) + dot_trans(up_delta, up_weight)
        wide = summed.shape[1]
        summed = exchange(summed.astype(BF16).reshape(nx, tokens // nx, wide), "x")
        summed = jnp.sum(summed.astype(F32), axis=0)
        summed = summed.reshape(far, near, tokens // (nx * far * near), wide)
        summed = jnp.sum(exchange(summed.transpose(1, 0, 2, 3), "zn"), axis=0)
        summed = jnp.sum(exchange(summed, ("zb", "zm")), axis=0).astype(BF16)

        down_grad = trans_dot(hidden, cols_grad).astype(BF16)
        gate_grad = trans_dot(cols_in, gate_delta).astype(BF16)
        up_grad = trans_dot(cols_in, up_delta).astype(BF16)
        return (summed, gate_grad, up_grad, down_grad)

    return shards


def build(mesh):
    return jax.shard_map(
        make_shards(mesh.shape),
        mesh=mesh,
        in_specs=(P(WID, None), P(WID, None), P(WID, HID), P(WID, HID), P(HID, WID)),
        out_specs=(P(HID, WID), P(WID, HID), P(WID, HID), P(HID, WID)),
        check_vma=False,
    )


def solution(mesh):
    return build(Mesh(mesh.devices.reshape(4, 2, 2, 4, 4, 2, 2), AXES))
```

```python
import jax
import jax.numpy as jnp
from jax import lax
from jax.sharding import Mesh, PartitionSpec as P

AXES = ("x", "zb", "zm", "zn", "y", "zhi", "core")
HID = ("x", "zb", "zm", "zn")
WID = ("y", "zhi", "core")
BF16 = jnp.bfloat16
F32 = jnp.float32


def trans_dot(left, right):
    return lax.dot_general(
        left, right, (((0,), (0,)), ((), ())), preferred_element_type=F32
    )


def dot_trans(left, right):
    return lax.dot_general(
        left, right, (((1,), (1,)), ((), ())), preferred_element_type=F32
    )


def nonlinear(gate, up, hidden_grad):
    sig = jax.nn.sigmoid(gate)
    hidden = (gate * sig * up).astype(BF16)
    gate_delta = (hidden_grad * up * sig * (1.0 + gate * (1.0 - sig))).astype(BF16)
    up_delta = (hidden_grad * gate * sig).astype(BF16)
    return jnp.stack([hidden, gate_delta, up_delta])


def exchange(value, axis):
    return lax.all_to_all(value, axis, 0, 0, tiled=True)


def flip(value, axis):
    return lax.ppermute(value, axis, [(0, 1), (1, 0)])


def spread(value, axis, size):
    return exchange(jnp.broadcast_to(value[None], (size, *value.shape)), axis)


def sum_near(value, axis, size):
    at = lax.axis_index(axis)
    total = lax.dynamic_index_in_dim(value, at, 0, keepdims=False)
    for step in range(size - 1, 0, -1):
        sent = lax.dynamic_index_in_dim(value, at ^ step, 0, keepdims=False)
        total = total + lax.ppermute(sent, axis, [(i, i ^ step) for i in range(size)])
    return total


def near_groups(ny, nc):
    return [
        [((g ^ h) * ny + y) * 2 * nc + h * nc + c for y in range(ny) for h in range(2) for c in range(nc)]
        for g in range(2)
    ]


def make_shards(sizes):
    nx, ny, nc = sizes["x"], sizes["y"], sizes["core"]
    far, near = sizes["zb"] * sizes["zm"], sizes["zn"]
    nw = ny * sizes["zhi"] * nc
    groups = near_groups(ny, nc)

    def shards(inputs, out_grad, gate_weight, up_weight, down_weight):
        at_x = lax.axis_index("x")
        at_core = lax.axis_index("core")
        own, width = inputs.shape
        cols = width // (nw * nx)
        tokens = own * nw
        hid = gate_weight.shape[1]

        both = jnp.stack([inputs, out_grad]).reshape(2, own, nw, nx, cols)
        quarter = lax.dynamic_index_in_dim(both, at_x, 3, keepdims=False)
        quarter = lax.all_to_all(
            quarter.transpose(2, 0, 1, 3), ("zb", *WID), 0, 0, axis_index_groups=groups, tiled=True
        )
        whole = spread(quarter, "x", nx)
        whole = whole.transpose(2, 1, 3, 0, 4).reshape(2, tokens, nx * cols)
        cols_in, cols_grad = whole[0], whole[1]

        block = tokens // (nc * ny)

        def pack(part):
            part = part.reshape(*part.shape[:-2], 2, block // 2, hid)
            return jnp.concatenate([part[..., 0, :, :], part[..., 1, :, :]], axis=-1)

        def products(core):
            rows_in = lax.dynamic_index_in_dim(cols_in.reshape(nc, tokens // nc, -1), core, 0, keepdims=False)
            rows_grad = lax.dynamic_index_in_dim(cols_grad.reshape(nc, tokens // nc, -1), core, 0, keepdims=False)
            parts = [
                jnp.dot(rows_in, gate_weight, preferred_element_type=F32),
                jnp.dot(rows_in, up_weight, preferred_element_type=F32),
                dot_trans(rows_grad, down_weight),
            ]
            return jnp.stack([pack(part.reshape(ny, block, hid)) for part in parts], axis=1)

        chip = flip(products(1 - at_core), "core") + products(at_core)
        half = jnp.sum(exchange(chip, "y"), axis=0)
        full = half + flip(half.astype(BF16), "zhi").astype(F32)

        deltas = spread(nonlinear(full[0], full[1], full[2]), "y", ny)
        other = flip(deltas, "core")
        first = jnp.where(at_core == 0, deltas, other)
        second = jnp.where(at_core == 0, other, deltas)
        deltas = jnp.stack([first, second]).transpose(2, 0, 1, 3, 4)
        deltas = jnp.stack([deltas[..., :hid], deltas[..., hid:]], axis=3).reshape(3, tokens, hid)
        hidden, gate_delta, up_delta = deltas[0], deltas[1], deltas[2]

        summed = dot_trans(gate_delta, gate_weight) + dot_trans(up_delta, up_weight)
        wide = summed.shape[1]
        summed = exchange(summed.astype(BF16).reshape(nx, tokens // nx, wide), "x")
        summed = jnp.sum(summed.astype(F32), axis=0)
        summed = summed.reshape(far, near, tokens // (nx * far * near), wide)
        down_grad = trans_dot(hidden, cols_grad).astype(BF16)
        gate_grad = trans_dot(cols_in, gate_delta).astype(BF16)
        up_grad = trans_dot(cols_in, up_delta).astype(BF16)
        summed = sum_near(summed.transpose(1, 0, 2, 3).reshape(near, -1, wide), "zn", near)
        summed, down_grad, gate_grad, up_grad = lax.optimization_barrier(
            (summed, down_grad, gate_grad, up_grad)
        )
        summed = exchange(summed.reshape(far, -1, wide), ("zb", "zm"))
        summed = jnp.sum(summed, axis=0).astype(BF16)

        return (summed, gate_grad, up_grad, down_grad)

    return shards


def build(mesh):
    return jax.shard_map(
        make_shards(mesh.shape),
        mesh=mesh,
        in_specs=(P(WID, None), P(WID, None), P(WID, HID), P(WID, HID), P(HID, WID)),
        out_specs=(P(HID, WID), P(WID, HID), P(WID, HID), P(HID, WID)),
        check_vma=False,
    )


def solution(mesh):
    return build(Mesh(mesh.devices.reshape(4, 2, 2, 4, 4, 2, 2), AXES))
```

```python
import jax
import jax.numpy as jnp
from jax import lax
from jax.sharding import Mesh, PartitionSpec as P

AXES = ("x", "zb", "zm", "zn", "y", "zhi", "core")
HID = ("x", "zb", "zm", "zn")
WID = ("y", "zhi", "core")
BF16 = jnp.bfloat16
F32 = jnp.float32


def trans_dot(left, right):
    return lax.dot_general(
        left, right, (((0,), (0,)), ((), ())), preferred_element_type=F32
    )


def dot_trans(left, right):
    return lax.dot_general(
        left, right, (((1,), (1,)), ((), ())), preferred_element_type=F32
    )


def nonlinear(gate, up, hidden_grad):
    sig = jax.nn.sigmoid(gate)
    hidden = (gate * sig * up).astype(BF16)
    gate_delta = (hidden_grad * up * sig * (1.0 + gate * (1.0 - sig))).astype(BF16)
    up_delta = (hidden_grad * gate * sig).astype(BF16)
    return jnp.stack([hidden, gate_delta, up_delta])


def exchange(value, axis):
    return lax.all_to_all(value, axis, 0, 0, tiled=True)


def flip(value, axis):
    return lax.ppermute(value, axis, [(0, 1), (1, 0)])


def spread(value, axis, size):
    return exchange(jnp.broadcast_to(value[None], (size, *value.shape)), axis)


def sum_near(value, axis, size):
    at = lax.axis_index(axis)
    total = lax.dynamic_index_in_dim(value, at, 0, keepdims=False)
    for step in range(size - 1, 0, -1):
        sent = lax.dynamic_index_in_dim(value, at ^ step, 0, keepdims=False)
        total = total + lax.ppermute(sent, axis, [(i, i ^ step) for i in range(size)])
    return total


def near_groups(ny, nc):
    return [
        [((g ^ h) * ny + y) * 2 * nc + h * nc + c for y in range(ny) for h in range(2) for c in range(nc)]
        for g in range(2)
    ]


def make_shards(sizes):
    nx, ny, nc = sizes["x"], sizes["y"], sizes["core"]
    far, near = sizes["zb"] * sizes["zm"], sizes["zn"]
    nw = ny * sizes["zhi"] * nc
    groups = near_groups(ny, nc)

    def shards(inputs, out_grad, gate_weight, up_weight, down_weight):
        at_x = lax.axis_index("x")
        at_core = lax.axis_index("core")
        own, width = inputs.shape
        cols = width // (nw * nx)
        tokens = own * nw
        hid = gate_weight.shape[1]

        both = jnp.stack([inputs, out_grad]).reshape(2, own, nw, nx, cols)
        quarter = lax.dynamic_index_in_dim(both, at_x, 3, keepdims=False)
        quarter = lax.all_to_all(
            quarter.transpose(2, 0, 1, 3), ("zb", *WID), 0, 0, axis_index_groups=groups, tiled=True
        )
        whole = spread(quarter, "x", nx)
        whole = whole.transpose(2, 1, 3, 0, 4).reshape(2, tokens, nx * cols)
        cols_in, cols_grad = whole[0], whole[1]

        block = tokens // (nc * ny)

        def pack(part):
            part = part.reshape(*part.shape[:-2], 2, block // 2, hid)
            return jnp.concatenate([part[..., 0, :, :], part[..., 1, :, :]], axis=-1)

        def products(core):
            rows_in = lax.dynamic_index_in_dim(cols_in.reshape(nc, tokens // nc, -1), core, 0, keepdims=False)
            rows_grad = lax.dynamic_index_in_dim(cols_grad.reshape(nc, tokens // nc, -1), core, 0, keepdims=False)
            parts = [
                jnp.dot(rows_in, gate_weight, preferred_element_type=F32),
                jnp.dot(rows_in, up_weight, preferred_element_type=F32),
                dot_trans(rows_grad, down_weight),
            ]
            return jnp.stack([pack(part.reshape(ny, block, hid)) for part in parts], axis=1)

        chip = flip(products(1 - at_core), "core") + products(at_core)
        half = jnp.sum(exchange(chip, "y"), axis=0)
        full = half + flip(half.astype(BF16), "zhi").astype(F32)

        deltas = spread(nonlinear(full[0], full[1], full[2]), "y", ny)
        other = flip(deltas, "core")
        first = jnp.where(at_core == 0, deltas, other)
        second = jnp.where(at_core == 0, other, deltas)
        deltas = jnp.stack([first, second]).transpose(2, 0, 1, 3, 4)
        deltas = jnp.stack([deltas[..., :hid], deltas[..., hid:]], axis=3).reshape(3, tokens, hid)
        hidden, gate_delta, up_delta = deltas[0], deltas[1], deltas[2]

        summed = dot_trans(gate_delta, gate_weight) + dot_trans(up_delta, up_weight)
        wide = summed.shape[1]
        summed = exchange(summed.astype(BF16).reshape(nx, tokens // nx, wide), "x")
        summed = jnp.sum(summed.astype(F32), axis=0)
        summed = summed.reshape(far, near, tokens // (nx * far * near), wide)
        down_grad = trans_dot(hidden, cols_grad).astype(BF16)
        gate_grad = trans_dot(cols_in, gate_delta).astype(BF16)
        up_grad = trans_dot(cols_in, up_delta).astype(BF16)
        summed = sum_near(summed.transpose(1, 0, 2, 3).reshape(near, -1, wide), "zn", near)
        summed, down_grad, gate_grad, up_grad = lax.optimization_barrier(
            (summed, down_grad, gate_grad, up_grad)
        )
        summed = summed.reshape(far, -1, wide)
        rows = summed.shape[1]
        summed = jnp.pad(summed, ((0, 0), (0, -rows % 8), (0, 0)))
        summed = jnp.sum(exchange(summed, ("zb", "zm")), axis=0)[:rows].astype(BF16)

        return (summed, gate_grad, up_grad, down_grad)

    return shards


def build(mesh):
    return jax.shard_map(
        make_shards(mesh.shape),
        mesh=mesh,
        in_specs=(P(WID, None), P(WID, None), P(WID, HID), P(WID, HID), P(HID, WID)),
        out_specs=(P(HID, WID), P(WID, HID), P(WID, HID), P(HID, WID)),
        check_vma=False,
    )


def solution(mesh):
    return build(Mesh(mesh.devices.reshape(4, 2, 2, 4, 4, 2, 2), AXES))
```

```python
import jax
import jax.numpy as jnp
from jax import lax
from jax.sharding import Mesh, PartitionSpec as P

AXES = ("x", "zb", "zm", "zn", "za", "y", "zhi", "core")
HID = ("x", "zb", "zm", "zn", "za")
NEAR = ("zn", "za")
WID = ("y", "zhi", "core")
BF16 = jnp.bfloat16
F32 = jnp.float32


def trans_dot(left, right):
    return lax.dot_general(
        left, right, (((0,), (0,)), ((), ())), preferred_element_type=F32
    )


def dot_trans(left, right):
    return lax.dot_general(
        left, right, (((1,), (1,)), ((), ())), preferred_element_type=F32
    )


def nonlinear(gate, up, hidden_grad):
    sig = jax.nn.sigmoid(gate)
    hidden = (gate * sig * up).astype(BF16)
    gate_delta = (hidden_grad * up * sig * (1.0 + gate * (1.0 - sig))).astype(BF16)
    up_delta = (hidden_grad * gate * sig).astype(BF16)
    return jnp.stack([hidden, gate_delta, up_delta])


def exchange(value, axis):
    return lax.all_to_all(value, axis, 0, 0, tiled=True)


def flip(value, axis):
    return lax.ppermute(value, axis, [(0, 1), (1, 0)])


def spread(value, axis, size):
    return exchange(jnp.broadcast_to(value[None], (size, *value.shape)), axis)


def sum_near(value, axis, size):
    at = lax.axis_index(axis)
    total = lax.dynamic_index_in_dim(value, at, 0, keepdims=False)
    for step in range(size - 1, 0, -1):
        sent = lax.dynamic_index_in_dim(value, at ^ step, 0, keepdims=False)
        total = total + lax.ppermute(sent, axis, [(i, i ^ step) for i in range(size)])
    return total


def near_groups(ny, nc):
    return [
        [((g ^ h) * ny + y) * 2 * nc + h * nc + c for y in range(ny) for h in range(2) for c in range(nc)]
        for g in range(2)
    ]


def make_shards(sizes):
    nx, ny, nc = sizes["x"], sizes["y"], sizes["core"]
    far, near = sizes["zb"] * sizes["zm"], sizes["zn"] * sizes["za"]
    nw = ny * sizes["zhi"] * nc
    groups = near_groups(ny, nc)

    def shards(inputs, out_grad, gate_weight, up_weight, down_weight):
        at_x = lax.axis_index("x")
        at_core = lax.axis_index("core")
        own, width = inputs.shape
        cols = width // (nw * nx)
        tokens = own * nw
        hid = gate_weight.shape[1]

        both = jnp.stack([inputs, out_grad]).reshape(2, own, nw, nx, cols)
        quarter = both[lax.axis_index("za"), :, :, at_x]
        quarter = lax.all_to_all(
            quarter.transpose(1, 0, 2), ("zb", *WID), 0, 0, axis_index_groups=groups, tiled=True
        )
        whole = spread(quarter, ("x", "za"), 2 * nx).reshape(nx, 2, nw, own, cols)
        whole = whole.transpose(1, 2, 3, 0, 4).reshape(2, tokens, nx * cols)
        cols_in, cols_grad = whole[0], whole[1]

        block = tokens // (nc * ny)

        def pack(part):
            part = part.reshape(*part.shape[:-2], 2, block // 2, hid)
            return jnp.concatenate([part[..., 0, :, :], part[..., 1, :, :]], axis=-1)

        def products(core):
            rows_in = lax.dynamic_index_in_dim(cols_in.reshape(nc, tokens // nc, -1), core, 0, keepdims=False)
            rows_grad = lax.dynamic_index_in_dim(cols_grad.reshape(nc, tokens // nc, -1), core, 0, keepdims=False)
            parts = [
                jnp.dot(rows_in, gate_weight, preferred_element_type=F32),
                jnp.dot(rows_in, up_weight, preferred_element_type=F32),
                dot_trans(rows_grad, down_weight),
            ]
            return jnp.stack([pack(part.reshape(ny, block, hid)) for part in parts], axis=1)

        chip = flip(products(1 - at_core), "core") + products(at_core)
        half = jnp.sum(exchange(chip, "y"), axis=0)
        full = half + flip(half.astype(BF16), "zhi").astype(F32)

        deltas = spread(nonlinear(full[0], full[1], full[2]), "y", ny)
        other = flip(deltas, "core")
        first = jnp.where(at_core == 0, deltas, other)
        second = jnp.where(at_core == 0, other, deltas)
        deltas = jnp.stack([first, second]).transpose(2, 0, 1, 3, 4)
        deltas = jnp.stack([deltas[..., :hid], deltas[..., hid:]], axis=3).reshape(3, tokens, hid)
        hidden, gate_delta, up_delta = deltas[0], deltas[1], deltas[2]

        summed = dot_trans(gate_delta, gate_weight) + dot_trans(up_delta, up_weight)
        wide = summed.shape[1]
        summed = exchange(summed.astype(BF16).reshape(nx, tokens // nx, wide), "x")
        summed = jnp.sum(summed.astype(F32), axis=0)
        summed = summed.reshape(far, near, tokens // (nx * far * near), wide)
        down_grad = trans_dot(hidden, cols_grad).astype(BF16)
        gate_grad = trans_dot(cols_in, gate_delta).astype(BF16)
        up_grad = trans_dot(cols_in, up_delta).astype(BF16)
        summed = sum_near(summed.transpose(1, 0, 2, 3).reshape(near, -1, wide), NEAR, near)
        summed, down_grad, gate_grad, up_grad = lax.optimization_barrier(
            (summed, down_grad, gate_grad, up_grad)
        )
        summed = exchange(summed.reshape(far, -1, wide), ("zb", "zm"))
        summed = jnp.sum(summed, axis=0).astype(BF16)

        return (summed, gate_grad, up_grad, down_grad)

    return shards


def build(mesh):
    return jax.shard_map(
        make_shards(mesh.shape),
        mesh=mesh,
        in_specs=(P(WID, None), P(WID, None), P(WID, HID), P(WID, HID), P(HID, WID)),
        out_specs=(P(HID, WID), P(WID, HID), P(WID, HID), P(HID, WID)),
        check_vma=False,
    )


def solution(mesh):
    return build(Mesh(mesh.devices.reshape(4, 2, 2, 2, 2, 4, 2, 2), AXES))
```
